32 devices in a mesh: clip: 8 (over z, y), tile: 4 (over x, core).
Axes of the slice: x: 2, y: 2, z: 4, core: 2. Of those that a mesh axis runs over, the one named last changes fastest.
Arguments:
- codes: int32 [8, 16, 256], P('clip', None, 'tile'), may hold values from 0 to 1023
- mask: int32 [8, 16, 256], P('clip', None, 'tile'), may hold values 0 or 1
- actions: int32 [8, 16], P('clip'), may hold values from 0 to 7
- domains: int32 [8], P('clip'), may hold values from 0 to 3
- weights: float32 [1024, 18432], P('clip')
- weight_m: float32 [1024, 18432], P('clip'), may hold values from -0.00015258789 to 0.00015258789
- weight_v: float32 [1024, 18432], P('clip'), may hold values from 2.7842804e-09 to 1.1115948e-08
- stats: float32 [8, 1024, 64], P(None, 'clip'), as said below
- bases: float32 [8, 1024, 64], P(None, 'clip'), as said below
- vectors: float32 [17, 1024], P(None, 'clip')
- vector_m: float32 [17, 1024], P(None, 'clip'), may hold values from -0.00061035156 to 0.00061035156
- vector_v: float32 [17, 1024], P(None, 'clip'), may hold values from 4.4463793e-08 to 1.7997249e-07
Outputs:
- loss_terms: float32 [2, 4], replicated
- grad_norm: float32 [], replicated
- new_weights: float32 [1024, 18432], P('clip')
- new_weight_m: float32 [1024, 18432], P('clip')
- new_weight_v: float32 [1024, 18432], P('clip')
- new_stats: float32 [8, 1024, 64], P(None, 'clip')
- new_bases: float32 [8, 1024, 64], P(None, 'clip')
- new_vectors: float32 [17, 1024], P(None, 'clip')
- new_vector_m: float32 [17, 1024], P(None, 'clip')
- new_vector_v: float32 [17, 1024], P(None, 'clip')
The draws below stay inside these ranges and needn't reach their ends.
Inputs may be any that keep to these rules, and one draw needn't show every extreme that they name: `stats`: symmetric, diagonally dominant 64 x 64 blocks with positive diagonal. `bases`: each 64 x 64 block is orthonormal.
All inputs are finite; a program needn't handle non-finite values. No bound on the sum of `mask` on one device may be relied on, other than what follows from the above.
Results may differ from the reference program's by a relative error of at most 0.012.
The reference program's roundings to bfloat16 on the way count: a program that leaves them out, or rounds other values in their place, can miss the bound.
Values may be sent and summed in bfloat16 or wider, within the bound.
No kernel may reach another device: no remote copies, remote signals or barrier semaphores. Data moves between devices by JAX's collectives and lax.ppermute only.
A program may use at most 384 MiB of HBM per device.

```python
import math
import jax
import jax.numpy as jnp
from jax import lax

D = 1024
HEADS = 16
HEAD = 64
FF = 4096
V = 1024
ACTIONS = 8
FRAMES = 16
GRID = 16
NDOM = 4
BLOCK = 64
STEP = 10
CLIPS = 8
POS = 256
VEC = 17
WCOLS = 18432


def slab_widths_drawn():
    return [3 * D, D, 3 * D, D, FF, FF, V, V]


def draw_weights(key, part):
    key = jax.random.fold_in(key, 11)
    factors = [D ** (-0.5), 3.0 * D ** (-0.5), D ** (-0.5), 2.0 * D ** (-0.5), D ** (-0.5), 1.5 * FF ** (-0.5), 1.0, D ** (-0.5)]
    pieces = []
    for extent, factor in zip(slab_widths_drawn(), factors):
        pieces.append(jnp.full((extent,), factor, jnp.float32))
    column_scale = jnp.concatenate(pieces)
    drawn = jax.random.normal(key, (D, WCOLS), jnp.float32)
    return drawn * column_scale[None, :]


def draw_stats(key, part):
    key = jax.random.fold_in(key, 12)
    first_key, second_key = jax.random.split(key)
    blocks = D // BLOCK
    param_total = D * WCOLS + VEC * D
    scales = jnp.array([0.0526 * extent / param_total for extent in slab_widths_drawn()], jnp.float32)
    diagonal = jax.random.uniform(first_key, (8, blocks, BLOCK), jnp.float32, 1.0, 4.0)
    noise = jax.random.uniform(second_key, (8, blocks, BLOCK, BLOCK), jnp.float32, -0.007, 0.007)
    mirrored = noise + jnp.swapaxes(noise, 2, 3)
    identity = (jnp.arange(BLOCK)[:, None] == jnp.arange(BLOCK)[None, :]).astype(jnp.float32)
    matrix = mirrored * (1.0 - identity) + identity * diagonal[..., None]
    return (matrix * scales[:, None, None, None]).reshape(8, D, BLOCK)


def draw_bases(key, part):
    key = jax.random.fold_in(key, 13)
    first_key, second_key = jax.random.split(key)
    blocks = D // BLOCK
    index = jnp.arange(BLOCK)
    joined = index[:, None] & index[None, :]
    parity = jnp.zeros((BLOCK, BLOCK), jnp.int32)
    for position in range(12):
        parity = parity + (joined >> position & 1)
    hadamard = (1 - 2 * (parity % 2)).astype(jnp.float32) / math.sqrt(BLOCK)
    signs = jnp.where(jax.random.bernoulli(first_key, 0.5, (8, blocks, 1, BLOCK)), 1.0, -1.0)
    rotated = hadamard[None, None] * signs
    vector = jax.random.normal(second_key, (8, blocks, BLOCK), jnp.float32)
    length = jnp.sum(vector * vector, -1)
    across = jnp.einsum('abi,abij->abj', vector, rotated, precision=lax.Precision.HIGHEST)
    basis = rotated - 2.0 * vector[..., :, None] * across[..., None, :] / length[..., None, None]
    return basis.reshape(8, D, BLOCK)


def draw_vectors(key, part):
    key = jax.random.fold_in(key, 14)
    key_set = jax.random.split(key, 3)
    rising = 0.6 + 1.2 * jnp.arange(D, dtype=jnp.float32) / D
    gains = rising[None, :] * jax.random.uniform(key_set[0], (4, D), jnp.float32, 0.7, 1.3)
    offsets = 0.3 * jax.random.normal(key_set[1], (4, D), jnp.float32)
    tables = 0.7 * jax.random.normal(key_set[2], (1 + ACTIONS, D), jnp.float32)
    return jnp.concatenate([gains, offsets, tables], 0)


def plant(values, stream_key, smallest, largest):
    place = [jax.random.randint(jax.random.fold_in(stream_key, axis), (), 0, length) for axis, length in enumerate(values.shape)]
    main_axis = values.shape.index(max(values.shape))
    neighbour = place[:main_axis] + [(place[main_axis] + 1) % values.shape[main_axis]] + place[main_axis + 1:]
    return values.at[tuple(place)].set(smallest).at[tuple(neighbour)].set(largest)


def levels(stream_key, shape, shards, low, top_value):
    gain = 1.0
    for dim, blocks in shards:
        heights = jax.random.uniform(jax.random.fold_in(jax.random.fold_in(stream_key, 6), dim), (blocks,), jnp.float32, low / len(shards), top_value / len(shards))
        gain = gain * jnp.repeat(jnp.exp(heights), shape[dim] // blocks).reshape((-1,) + (1,) * (len(shape) - 1 - dim))
    return gain


def bell_draw(own_key, dims, width, most, cuts=(), kind=jnp.bfloat16):
    factor_of = levels(own_key, dims, cuts, -0.22, 0.18) if cuts else 1.0
    result = jax.random.normal(own_key, dims, jnp.float32) * width * factor_of
    return jnp.minimum(jnp.maximum(result, -most), most).astype(kind)


def setup_inputs(seed: int = 0) -> dict:
    splits = jax.random.split(jax.random.key(seed), 13)
    return {
        "codes": plant(jax.random.randint(splits[0], (CLIPS, FRAMES, POS), 0, V), jax.random.fold_in(splits[0], 1), 0, V - 1).astype(jnp.int32),
        "mask": plant((jax.random.randint(splits[1], (CLIPS, FRAMES, POS), 0, 2) < 1).astype(jnp.int32), jax.random.fold_in(splits[1], 1), 0, 1),
        "actions": plant(jax.random.randint(splits[2], (CLIPS, FRAMES), 0, ACTIONS), jax.random.fold_in(splits[2], 1), 0, ACTIONS - 1).astype(jnp.int32),
        "domains": plant(jax.random.randint(splits[3], (CLIPS,), 0, NDOM), jax.random.fold_in(splits[3], 1), 0, NDOM - 1).astype(jnp.int32),
        "weights": draw_weights(jax.random.fold_in(splits[12], 71), 0),
        "weight_m": bell_draw(splits[5], (D, WCOLS), (0.111 / (D * WCOLS + VEC * D) ** 0.5), 0.00015258789, ((0, 8),), jnp.float32),
        "weight_v": jnp.clip(jnp.exp(math.log(1.1115948161943834e-08) - 1.3843914 * jax.random.uniform(splits[6], (D, WCOLS), jnp.float32) ** levels(splits[6], (D, WCOLS), ((0, 8),), -0.2, 0.2)), 2.7842803618227663e-09, 1.1115948161943834e-08),
        "stats": draw_stats(jax.random.fold_in(splits[12], 71), 0),
        "bases": draw_bases(jax.random.fold_in(splits[12], 71), 0),
        "vectors": draw_vectors(jax.random.fold_in(splits[12], 71), 0),
        "vector_m": bell_draw(splits[10], (VEC, D), (0.444 / (D * WCOLS + VEC * D) ** 0.5), 0.00061035156, ((1, 8),), jnp.float32),
        "vector_v": jnp.clip(jnp.exp(math.log(1.7997248846768343e-07) - 1.3981288 * jax.random.uniform(splits[11], (VEC, D), jnp.float32) ** levels(splits[11], (VEC, D), ((1, 8),), -0.2, 0.2)), 4.4463792647775335e-08, 1.7997248846768343e-07),
    }


highest = lax.Precision.HIGHEST
eps_norm = 1e-05
beta_first = 0.9
beta_second = 0.95
beta_stats = 0.95
rate_matrix = 0.2
rate_vector = 0.2
weight_decay = 0.01
eps_adam = 1e-08
masked_score = -1e+30

@jax.custom_vjp
def low(v):
    return lax.optimization_barrier(v.astype(jnp.bfloat16)).astype(jnp.float32)

@jax.custom_vjp
def low_back(v):
    return v

def low_keep(v):
    return (low(v), None)

def low_pass(kept, grad):
    return (grad,)

def back_keep(v):
    return (v, None)

def back_low(kept, grad):
    return (low(grad),)
low.defvjp(low_keep, low_pass)
low_back.defvjp(back_keep, back_low)

def both_ways(tensor):
    return low_back(low(tensor))

def matmul(former, latter):
    return jnp.dot(former, latter, precision=highest)

def slab_widths():
    return [3 * D, D, 3 * D, D, FF, FF, V, V]

def slab_starts():
    starts = [0]
    for extent in slab_widths():
        starts.append(starts[-1] + extent)
    return starts

def layer_norm(inputs, gains, offset):
    center = inputs - lax.optimization_barrier(jnp.mean(inputs, -1, keepdims=True))
    spread = lax.optimization_barrier(jnp.mean(center * center, -1, keepdims=True))
    return center * lax.rsqrt(spread + eps_norm) * gains + offset

def clip_loss(weight_all, vector_all, clip_codes, clip_mask, clip_actions, clip_domain, inverse):
    starts = slab_starts()
    slabs = [weight_all[:, starts[number]:starts[number + 1]] for number in range(8)]
    token_rows = FRAMES * GRID * GRID
    code_hot = (clip_codes.reshape(token_rows)[:, None] == jnp.arange(V)[None, :]).astype(jnp.float32)
    mask_col = clip_mask.reshape(token_rows, 1).astype(jnp.float32)
    action_hot = (clip_actions[:, None] == jnp.arange(ACTIONS)[None, :]).astype(jnp.float32)
    action_add = matmul(action_hot, vector_all[9:])
    looked = low_back(matmul(code_hot, slabs[6].T))
    stream = mask_col * vector_all[8] + (1.0 - mask_col) * looked + jnp.repeat(action_add, GRID * GRID, axis=0)
    normed = low(layer_norm(stream, vector_all[0], vector_all[4]))
    projected = both_ways(matmul(normed, slabs[0])).reshape(FRAMES, GRID * GRID, 3, HEADS, HEAD)
    scores = low_back(jnp.einsum('fqhe,fkhe->fhqk', projected[:, :, 0], projected[:, :, 1], precision=highest) * 0.125)
    attn_prob = low(jax.nn.softmax(scores, axis=-1))
    attended = both_ways(jnp.einsum('fhqk,fkhe->fqhe', attn_prob, projected[:, :, 2], precision=highest).reshape(token_rows, D))
    stream = stream + low_back(matmul(attended, slabs[1]))
    normed = low(layer_norm(stream, vector_all[1], vector_all[5]))
    projected = both_ways(matmul(normed, slabs[2])).reshape(FRAMES, GRID * GRID, 3, HEADS, HEAD)
    scores = low_back(jnp.einsum('fphe,gphe->phfg', projected[:, :, 0], projected[:, :, 1], precision=highest) * 0.125)
    allowed = jnp.arange(FRAMES)[:, None] >= jnp.arange(FRAMES)[None, :]
    attn_prob = low(jax.nn.softmax(jnp.where(allowed, scores, masked_score), axis=-1))
    attended = both_ways(jnp.einsum('phfg,gphe->fphe', attn_prob, projected[:, :, 2], precision=highest).reshape(token_rows, D))
    stream = stream + low_back(matmul(attended, slabs[3]))
    normed = low(layer_norm(stream, vector_all[2], vector_all[6]))
    hidden_up = low_back(matmul(normed, slabs[4]))
    activated = low(jax.nn.gelu(hidden_up, approximate=False))
    stream = stream + low_back(matmul(activated, slabs[5].T))
    normed = low(layer_norm(stream, vector_all[3], vector_all[7]))
    logits = low_back(matmul(normed, slabs[7]))
    log_sum = jax.nn.logsumexp(logits, axis=-1)
    picked = lax.optimization_barrier(jnp.sum(logits * code_hot, -1))
    clip_total = jnp.sum((log_sum - picked) * mask_col[:, 0])
    domain_hot = (jnp.arange(NDOM) == clip_domain).astype(jnp.float32)
    return (clip_total * jnp.sum(domain_hot * inverse) / NDOM, clip_total * domain_hot)

def soap_update(weights, moment, second, stats, bases, grad):
    new_moment = beta_first * moment + (1.0 - beta_first) * grad
    first_fix = 1.0 - beta_first ** STEP
    second_fix = 1.0 - beta_second ** STEP
    starts = slab_starts()
    blocks = weights.shape[0] // BLOCK
    weight_list, second_list, stat_list, basis_list = ([], [], [], [])
    for number in range(8):
        begin = starts[number]
        finish = starts[number + 1]
        block_shape = (blocks, BLOCK, finish - begin)
        grad_block = grad[:, begin:finish].reshape(block_shape)
        moment_block = new_moment[:, begin:finish].reshape(block_shape)
        weight_block = weights[:, begin:finish].reshape(block_shape)
        basis = bases[number].reshape(blocks, BLOCK, BLOCK)
        stat = stats[number].reshape(blocks, BLOCK, BLOCK)
        grad_rot = jnp.einsum('bki,bkc->bic', basis, grad_block, precision=highest)
        moment_rot = jnp.einsum('bki,bkc->bic', basis, moment_block, precision=highest)
        second_new = beta_second * second[:, begin:finish].reshape(block_shape) + (1.0 - beta_second) * grad_rot * grad_rot
        direction = moment_rot / first_fix / (jnp.sqrt(second_new / second_fix) + eps_adam)
        stepped = jnp.einsum('bik,bkc->bic', basis, direction, precision=highest)
        weight_new = weight_block - rate_matrix * (stepped + weight_decay * weight_block)
        stat_new = beta_stats * stat + (1.0 - beta_stats) * jnp.einsum('bic,bkc->bik', grad_block, grad_block, precision=highest)
        turned = jnp.einsum('bik,bkj->bij', stat_new, basis, precision=highest)
        gram = jnp.einsum('bki,bkj->bij', turned, turned, precision=highest)
        factor = jnp.linalg.cholesky(gram)
        basis_new = jnp.swapaxes(lax.linalg.triangular_solve(factor, jnp.swapaxes(turned, 1, 2), left_side=True, lower=True), 1, 2)
        weight_list.append(weight_new.reshape(blocks * BLOCK, finish - begin))
        second_list.append(second_new.reshape(blocks * BLOCK, finish - begin))
        stat_list.append(stat_new.reshape(blocks * BLOCK, BLOCK))
        basis_list.append(basis_new.reshape(blocks * BLOCK, BLOCK))
    return (jnp.concatenate(weight_list, 1), new_moment, jnp.concatenate(second_list, 1), jnp.stack(stat_list), jnp.stack(basis_list))

def adam_update(values, moment, second, grad):
    new_moment = beta_first * moment + (1.0 - beta_first) * grad
    new_second = beta_second * second + (1.0 - beta_second) * grad * grad
    corrected = new_moment / (1.0 - beta_first ** STEP) / (jnp.sqrt(new_second / (1.0 - beta_second ** STEP)) + eps_adam)
    return (values - rate_vector * corrected, new_moment, new_second)

def reference(codes, mask, actions, domains, weights, weight_m, weight_v, stats, bases, vectors, vector_m, vector_v):
    domain_hot = (domains[:, None] == jnp.arange(NDOM)[None, :]).astype(jnp.float32)
    counts = lax.optimization_barrier(jnp.sum(domain_hot * lax.optimization_barrier(jnp.sum(mask.astype(jnp.float32), axis=(1, 2)))[:, None], 0))
    inverse = 1.0 / jnp.maximum(counts, 1.0)

    def total_loss(weight_all, vector_all):
        weight_low = low(weight_all)
        vector_low = low(vector_all)
        checked = jax.checkpoint(clip_loss)

        def per_clip(clip_items):
            return checked(weight_low, vector_low, clip_items[0], clip_items[1], clip_items[2], clip_items[3], inverse)
        losses, domain_terms = lax.map(per_clip, (codes, mask, actions, domains))
        return (jnp.sum(losses), lax.optimization_barrier(jnp.sum(domain_terms, 0)))
    unused, pullback, ce_total = jax.vjp(total_loss, weights, vectors, has_aux=True)
    grad_w, grad_v = pullback(jnp.ones((), jnp.float32))
    grad_norm = jnp.sqrt(jnp.sum(grad_w * grad_w) + jnp.sum(grad_v * grad_v))
    clip_scale = 1.0 / jnp.maximum(grad_norm, 1.0)
    new_weights, new_weight_m, new_weight_v, new_stats, new_bases = soap_update(weights, weight_m, weight_v, stats, bases, grad_w * clip_scale)
    new_vectors, new_vector_m, new_vector_v = adam_update(vectors, vector_m, vector_v, grad_v * clip_scale)
    loss_terms = jnp.stack([ce_total, counts])
    return (loss_terms, grad_norm, new_weights, new_weight_m, new_weight_v, new_stats, new_bases, new_vectors, new_vector_m, new_vector_v)
```

```python
from functools import partial

import jax
import jax.numpy as jnp
from jax import lax
from jax.experimental import pallas as pl
from jax.experimental.pallas import tpu as pltpu
from jax.sharding import PartitionSpec as P

D = 1024
HEADS = 16
HEAD = 64
FF = 4096
V = 1024
ACTIONS = 8
NDOM = 4
BLOCK = 64
STEP = 10
CORES = 2
LANES = 128
QUAD = 256
FOLD = 4


highest = lax.Precision.HIGHEST
eps_norm = 1e-05
beta_first = 0.9
beta_second = 0.95
beta_stats = 0.95
rate_matrix = 0.2
rate_vector = 0.2
weight_decay = 0.01
eps_adam = 1e-08
masked_score = -1e30
first_fix = 1.0 - beta_first**STEP
second_fix = 1.0 - beta_second**STEP

f32 = jnp.float32
bf16 = jnp.bfloat16

WIDTHS = [3 * D, D, 3 * D, D, FF, FF, V, V]
STARTS = [sum(WIDTHS[:number]) for number in range(9)]


def dot_nn(former, latter):
    return jnp.dot(former, latter, preferred_element_type=f32)


def dot_tn(former, latter):
    return lax.dot_general(former, latter, (((0,), (0,)), ((), ())), preferred_element_type=f32)


def dot_nt(former, latter):
    return lax.dot_general(former, latter, (((1,), (1,)), ((), ())), preferred_element_type=f32)


def norm_stats(inputs):
    mean = jnp.mean(inputs, -1, keepdims=True)
    center = inputs - mean
    spread = jnp.mean(center * center, -1, keepdims=True)
    return (mean, lax.rsqrt(spread + eps_norm))


def norm_apply(inputs, stat, gain, offset):
    mean, scale = stat
    return ((inputs - mean) * scale * gain + offset).astype(bf16)


def norm_back(inputs, stat, gain, grad_out):
    mean, scale = stat
    normal = (inputs - mean) * scale
    grad_gain = jnp.sum(grad_out * normal, 0)
    grad_offset = jnp.sum(grad_out, 0)
    error = grad_out * gain
    first = jnp.mean(error, -1, keepdims=True)
    second = jnp.mean(error * normal, -1, keepdims=True)
    return ((error - first - normal * second) * scale, grad_gain, grad_offset)


def gelu_pair(value):
    size = jnp.abs(value) * (0.5**0.5)
    ratio = 1.0 / (1.0 + 0.3275911 * size)
    bell = jnp.exp(-size * size)
    series = 1.061405429
    for term in (-1.453152027, 1.421413741, -0.284496736, 0.254829592):
        series = series * ratio + term
    tail = 0.5 * series * ratio * bell
    phi = jnp.where(value >= 0.0, 1.0 - tail, tail)
    return (value * phi, phi + value * bell * 0.3989422804014327)


def head_masks(rows):
    lane = lax.broadcasted_iota(jnp.int32, (rows, QUAD), 1) // HEAD
    return [lane == number for number in range(FOLD)]


def fold_heads(block):
    masks = head_masks(block.shape[0])
    zero = jnp.zeros_like(block)
    return jnp.concatenate([jnp.where(mask, block, zero) for mask in masks], 0)


def unfold_heads(stacked):
    rows = stacked.shape[0] // FOLD
    masks = head_masks(rows)
    total = jnp.where(masks[0], stacked[:rows], 0.0)
    for number in range(1, FOLD):
        total = jnp.where(masks[number], stacked[number * rows : (number + 1) * rows], total)
    return total


def allow_mask(shape, span, query_axis):
    query = lax.broadcasted_iota(jnp.int32, shape, query_axis)
    key = lax.broadcasted_iota(jnp.int32, shape, 1 - query_axis)
    if query_axis == 0:
        query = query % QUAD
    else:
        key = key % QUAD
    return (query % span == key % span) & (key // span <= query // span)


def attend_kernel(query_ref, key_ref, value_ref, out_ref, *, span):
    query = query_ref[...].reshape(QUAD, QUAD)
    key = key_ref[...].reshape(QUAD, QUAD)
    value = value_ref[...].reshape(QUAD, QUAD)
    scores = dot_nt(fold_heads(query), key) * 0.125
    if span:
        scores = jnp.where(allow_mask(scores.shape, span, 0), scores, masked_score)
    powers = jnp.exp(scores - jnp.max(scores, -1, keepdims=True))
    attn = (powers * (1.0 / jnp.sum(powers, -1, keepdims=True))).astype(bf16)
    mixed = unfold_heads(dot_nn(attn, value))
    out_ref[...] = mixed.astype(bf16).reshape(out_ref.shape)


def attend_back_kernel(
    query_ref, key_ref, value_ref, grad_ref, dquery_ref, dkey_ref, dvalue_ref, *, span
):
    query = query_ref[...].reshape(QUAD, QUAD)
    key = key_ref[...].reshape(QUAD, QUAD)
    value = value_ref[...].reshape(QUAD, QUAD)
    grad = grad_ref[...].reshape(QUAD, QUAD)
    key_fold = fold_heads(key)
    scores = dot_nt(key_fold, query) * 0.125
    if span:
        scores = jnp.where(allow_mask(scores.shape, span, 1), scores, masked_score)
    scores = scores.reshape(FOLD, QUAD, QUAD)
    powers = jnp.exp(scores - jnp.max(scores, 1, keepdims=True))
    attn = powers * (1.0 / jnp.sum(powers, 1, keepdims=True))
    grad_attn = dot_nt(fold_heads(value), grad).reshape(FOLD, QUAD, QUAD)
    delta = jnp.sum(grad_attn * attn, 1, keepdims=True)
    grad_score = (attn * (grad_attn - delta)).astype(bf16).reshape(FOLD * QUAD, QUAD)
    attn = attn.astype(bf16).reshape(FOLD * QUAD, QUAD)
    dvalue = unfold_heads(dot_nn(attn, grad))
    dkey = unfold_heads(dot_nn(grad_score, query)) * 0.125
    dquery = dot_tn(grad_score, key_fold) * 0.125
    dquery_ref[...] = dquery.astype(bf16).reshape(dquery_ref.shape)
    dkey_ref[...] = dkey.astype(bf16).reshape(dkey_ref.shape)
    dvalue_ref[...] = dvalue.astype(bf16).reshape(dvalue_ref.shape)


def attend_params():
    return pltpu.CompilerParams(
        vmem_limit_bytes=40 * 1024 * 1024, dimension_semantics=("arbitrary", "arbitrary")
    )


QUADS = D // QUAD


def space_spec(part):
    return pl.BlockSpec((QUAD, QUAD), lambda frame, quad, part=part: (frame, part * QUADS + quad))


def time_spec(part, span, frames):
    return pl.BlockSpec(
        (frames, span, QUAD), lambda group, quad, part=part: (0, group, part * QUADS + quad)
    )


def attend_space(projected):
    rows = projected.shape[0]
    return pl.pallas_call(
        partial(attend_kernel, span=0),
        grid=(rows // QUAD, QUADS),
        in_specs=[space_spec(0), space_spec(1), space_spec(2)],
        out_specs=space_spec(0),
        out_shape=jax.ShapeDtypeStruct((rows, D), bf16),
        compiler_params=attend_params(),
    )(projected, projected, projected)


def attend_space_back(projected, grad):
    rows = projected.shape[0]
    shape = jax.ShapeDtypeStruct((rows, D), bf16)
    parts = pl.pallas_call(
        partial(attend_back_kernel, span=0),
        grid=(rows // QUAD, QUADS),
        in_specs=[space_spec(0), space_spec(1), space_spec(2), space_spec(0)],
        out_specs=[space_spec(0)] * 3,
        out_shape=[shape] * 3,
        compiler_params=attend_params(),
    )(projected, projected, projected, grad)
    return jnp.concatenate(parts, -1)


def attend_time(projected, frames):
    rows = projected.shape[0]
    local = rows // frames
    span = QUAD // frames
    cube = projected.reshape(frames, local, 3 * D)
    return pl.pallas_call(
        partial(attend_kernel, span=span),
        grid=(local // span, QUADS),
        in_specs=[time_spec(part, span, frames) for part in range(3)],
        out_specs=time_spec(0, span, frames),
        out_shape=jax.ShapeDtypeStruct((frames, local, D), bf16),
        compiler_params=attend_params(),
    )(cube, cube, cube).reshape(rows, D)


def attend_time_back(projected, grad, frames):
    rows = projected.shape[0]
    local = rows // frames
    span = QUAD // frames
    cube = projected.reshape(frames, local, 3 * D)
    shape = jax.ShapeDtypeStruct((frames, local, D), bf16)
    parts = pl.pallas_call(
        partial(attend_back_kernel, span=span),
        grid=(local // span, QUADS),
        in_specs=[time_spec(part, span, frames) for part in range(3)]
        + [time_spec(0, span, frames)],
        out_specs=[time_spec(0, span, frames)] * 3,
        out_shape=[shape] * 3,
        compiler_params=attend_params(),
    )(cube, cube, cube, grad.reshape(frames, local, D))
    return jnp.concatenate([part.reshape(rows, D) for part in parts], -1)


class Level:
    def __init__(self, size, stride, total):
        self.size, self.stride, self.total = size, stride, total

    def digit(self):
        return (lax.axis_index(("clip", "tile")) // self.stride) % self.size

    def shift(self, array, step):
        pairs = []
        for source in range(self.total):
            digit = (source // self.stride) % self.size
            target = source + ((digit + step) % self.size - digit) * self.stride
            pairs.append((source, target))
        return lax.ppermute(array, ("clip", "tile"), pairs)

    def swap(self, array, flip):
        pairs = []
        for source in range(self.total):
            digit = (source // self.stride) % self.size
            pairs.append((source, source + ((digit ^ flip) - digit) * self.stride))
        return lax.ppermute(array, ("clip", "tile"), pairs)

    def sum(self, array):
        flip = 1
        while flip < self.size:
            array = array + self.swap(array, flip)
            flip *= 2
        return array


def make_levels(clips, tiles):
    total = clips * tiles
    across = tiles // CORES
    outer = 4 if clips % 4 == 0 else clips
    inner = clips // outer
    return {
        "core": Level(CORES, 1, total),
        "x": Level(across, CORES, total),
        "inner": Level(inner, tiles, total),
        "outer": Level(outer, tiles * inner, total),
    }


def cut(array, index, size, axis):
    return lax.dynamic_slice_in_dim(array, index * size, size, axis)


def assemble(level, pieces, axis):
    digit = level.digit()
    width = pieces[0].shape[axis]
    shape = list(pieces[0].shape)
    shape[axis] = width * level.size
    whole = jnp.zeros(shape, pieces[0].dtype)
    for step, piece in enumerate(pieces):
        place = (digit - step) % level.size
        whole = lax.dynamic_update_slice_in_dim(whole, piece, place * width, axis)
    return whole


def gather(level, piece, axis):
    pieces = [piece] + [level.shift(piece, step) for step in range(1, level.size)]
    return assemble(level, pieces, axis)


class Reducer:
    def __init__(self, levels):
        self.levels = levels
        self.core = levels["core"].digit()
        self.x = levels["x"].digit()
        self.inner = levels["inner"].digit()
        self.outer = levels["outer"].digit()

    def rows_of(self, former, inner):
        outer = self.levels["outer"].size
        count = self.levels["inner"].size
        rows = former.shape[-1] // (outer * count)
        split = former.reshape(former.shape[0], outer, count, rows)
        return lax.dynamic_index_in_dim(split, inner, 2, keepdims=False).reshape(
            former.shape[0], outer * rows
        )

    def row_cut(self, array, inner):
        outer = self.levels["outer"].size
        count = self.levels["inner"].size
        rows = array.shape[0] // (outer * count)
        split = array.reshape(outer, count, rows, array.shape[1])
        return lax.dynamic_index_in_dim(split, inner, 1, keepdims=False).reshape(
            outer * rows, array.shape[1]
        )

    def start(self, former, latter):
        width = latter.shape[1]
        across = self.levels["x"].size
        half, quarter = width // CORES, width // (CORES * across)
        other = cut(latter, 1 - self.core, half, 1)
        own = cut(latter, self.core, half, 1)
        from_core = self.levels["core"].shift(dot_tn(former, other).astype(bf16), 1)
        from_x = []
        for step in range(1, across):
            place = (self.x + step) % across
            part = dot_tn(former, cut(own, place, quarter, 1))
            part = part + cut(from_core, place, quarter, 1).astype(f32)
            from_x.append(self.levels["x"].shift(part.astype(bf16), step))
        kept = cut(own, self.x, quarter, 1)
        kept_core = cut(from_core, self.x, quarter, 1)

        def rows(inner):
            part = dot_tn(self.rows_of(former, inner), kept)
            for piece in [kept_core] + from_x:
                part = part + self.row_cut(piece, inner).astype(f32)
            return part

        return (quarter, rows)

    def start_vector(self, array):
        total = array
        for name in ("core", "x"):
            sent = total.astype(bf16)
            for step in range(1, self.levels[name].size):
                total = total + self.levels[name].shift(sent, step).astype(f32)

        def rows(inner):
            return self.row_cut(total, inner)

        return (array.shape[1], rows)

    def finish(self, started):
        inner, outer = self.levels["inner"], self.levels["outer"]
        from_inner = []
        for step in range(1, inner.size):
            place = (self.inner + step) % inner.size
            sent = jnp.concatenate([rows(place).astype(bf16) for _, rows in started], 1)
            from_inner.append(inner.shift(sent, step))
        total = jnp.concatenate([rows(self.inner) for _, rows in started], 1)
        for piece in from_inner:
            total = total + piece.astype(f32)
        count = total.shape[0] // outer.size
        low = total.astype(bf16)
        from_outer = []
        for step in range(1, outer.size):
            place = (self.outer + step) % outer.size
            from_outer.append(outer.shift(cut(low, place, count, 0), step))
        total = cut(total, self.outer, count, 0)
        for piece in from_outer:
            total = total + piece.astype(f32)
        return total

    def spread(self, quarters, sizes):
        low = quarters.astype(bf16)
        rows = low.shape[0]
        x, core = self.levels["x"], self.levels["core"]
        from_x = [low] + [x.shift(low, step) for step in range(1, x.size)]
        halves, begin = [], 0
        for size in sizes:
            halves.append(assemble(x, [piece[:, begin : begin + size] for piece in from_x], 1))
            begin += size
        half = jnp.concatenate(halves, 1)
        from_core = [half, core.shift(half, 1)]
        wholes, begin = [], 0
        for size in sizes:
            size = size * x.size
            wholes.append(assemble(core, [piece[:, begin : begin + size] for piece in from_core], 1))
            begin += size
        return wholes


def split_two(array):
    high = array.astype(bf16)
    return (high, (array - high.astype(f32)).astype(bf16))


def dot_three(left, right):
    return (
        dot_nn(left[0], right[0]) + dot_nn(left[1], right[0]) + dot_nn(left[0], right[1])
    )


def update_kernel(
    scale_ref, grad_ref, weight_ref, moment_ref, second_ref,
    turn_high_ref, turn_low_ref, back_high_ref, back_low_ref,
    new_weight_ref, new_moment_ref, new_second_ref,
):
    scale = scale_ref[0]
    grad = grad_ref[...]
    turn = (turn_high_ref[0], turn_low_ref[0])
    back = (back_high_ref[0], back_low_ref[0])
    moment = moment_ref[...]
    weight = weight_ref[...]
    grad_rot = (dot_nn(turn[0], grad) + dot_nn(turn[1], grad)) * scale
    new_moment_ref[...] = beta_first * moment + (1.0 - beta_first) * (grad.astype(f32) * scale)
    moment_rot = beta_first * dot_three(turn, split_two(moment)) + (1.0 - beta_first) * grad_rot
    second = beta_second * second_ref[...] + (1.0 - beta_second) * grad_rot * grad_rot
    new_second_ref[...] = second
    direction = (moment_rot * (1.0 / first_fix)) / (jnp.sqrt(second * (1.0 / second_fix)) + eps_adam)
    stepped = dot_three(back, split_two(direction))
    new_weight_ref[...] = weight - rate_matrix * (stepped + weight_decay * weight)


def matrix_of(chunk, size):
    number = 0
    for start in STARTS[1:8]:
        number = number + jnp.where(chunk * size >= start, 1, 0)
    return number


def update_weights(scale, grad, weights, moment, second, bases):
    rows, cols = weights.shape
    chunk = 1024
    blocks = rows // BLOCK
    square = bases.reshape(8, blocks, BLOCK, BLOCK)
    pick = jnp.eye(blocks, dtype=f32)
    wide = (square[:, :, :, None, :] * pick[None, :, None, :, None]).reshape(8, rows, rows)
    back = split_two(wide)
    turn = split_two(jnp.swapaxes(wide, 1, 2))
    slab = pl.BlockSpec((rows, chunk), lambda place: (0, place))
    basis = pl.BlockSpec((1, rows, rows), lambda place: (matrix_of(place, chunk), 0, 0))
    shape = jax.ShapeDtypeStruct((rows, cols), f32)
    return pl.pallas_call(
        update_kernel,
        grid=(cols // chunk,),
        in_specs=[pl.BlockSpec(memory_space=pltpu.SMEM)] + [slab] * 4 + [basis] * 4,
        out_specs=[slab] * 3,
        out_shape=[shape] * 3,
        compiler_params=pltpu.CompilerParams(
            vmem_limit_bytes=48 * 1024 * 1024, dimension_semantics=("arbitrary",)
        ),
    )(scale.reshape(1), grad, weights, moment, second, *turn, *back)


def dot_exact(former, latter, dims):
    return lax.dot_general(
        former, latter, (dims, ((), ())), precision=highest, preferred_element_type=f32
    )


def turn_kernel(scale_ref, outer_ref, stat_ref, basis_ref, new_stat_ref, new_basis_ref, work_ref):
    count = stat_ref.shape[0]
    scale = scale_ref[0]
    for number in range(count):
        stat = beta_stats * stat_ref[number] + (1.0 - beta_stats) * (
            scale * scale * outer_ref[number]
        )
        new_stat_ref[number] = stat
        turned = dot_exact(basis_ref[number], stat, ((0,), (1,)))
        gram = dot_exact(turned, turned, ((1,), (1,)))
        work_ref[number] = jnp.concatenate([gram, turned], 1)

    for stage in range(4):
        low = stage * (BLOCK // 4)
        shape = (count, BLOCK - low, 2 * BLOCK)
        lane = lax.broadcasted_iota(jnp.int32, shape, 2)
        line = lax.broadcasted_iota(jnp.int32, shape, 1) + low

        def step(place, carry, low=low, lane=lane, line=line):
            held = work_ref[:, low:, :]
            row = jnp.sum(jnp.where(line == place, held, 0.0), 1, keepdims=True)
            column = jnp.sum(jnp.where(lane == place, held, 0.0), 2, keepdims=True)
            pivot = jnp.sum(jnp.where(lane[:, :1] == place, row, 0.0), 2, keepdims=True)
            inverse = lax.rsqrt(pivot)
            row = row * inverse
            column = column * inverse
            done = held - column * row
            held = jnp.where(line > place, done, held)
            work_ref[:, low:, :] = jnp.where(line == place, row, held)
            return carry

        lax.fori_loop(low, low + BLOCK // 4, step, 0)

    for number in range(count):
        new_basis_ref[number] = jnp.transpose(work_ref[number])[BLOCK:, :]


def turn_bases(scale, outers, stats, bases):
    rows = stats.shape[1]
    count = 8 * rows // BLOCK
    cubes = [array.reshape(count, BLOCK, BLOCK) for array in (outers, stats, bases)]
    shape = jax.ShapeDtypeStruct((count, BLOCK, BLOCK), f32)
    new_stats, new_bases = pl.pallas_call(
        turn_kernel,
        in_specs=[pl.BlockSpec(memory_space=pltpu.SMEM)]
        + [pl.BlockSpec(memory_space=pltpu.VMEM)] * 3,
        out_specs=[pl.BlockSpec(memory_space=pltpu.VMEM)] * 2,
        out_shape=[shape] * 2,
        scratch_shapes=[pltpu.VMEM((count, BLOCK, 2 * BLOCK), f32)],
        compiler_params=pltpu.CompilerParams(vmem_limit_bytes=32 * 1024 * 1024),
    )(scale.reshape(1), *cubes)
    return (new_stats.reshape(8, rows, BLOCK), new_bases.reshape(8, rows, BLOCK))


def adam_update(values, moment, second, grad):
    new_moment = beta_first * moment + (1.0 - beta_first) * grad
    new_second = beta_second * second + (1.0 - beta_second) * grad * grad
    corrected = (
        new_moment
        / (1.0 - beta_first**STEP)
        / (jnp.sqrt(new_second / (1.0 - beta_second**STEP)) + eps_adam)
    )
    return (values - rate_vector * corrected, new_moment, new_second)


def body(
    sizes,
    codes,
    mask,
    actions,
    domains,
    weights,
    weight_m,
    weight_v,
    stats,
    bases,
    vectors,
    vector_m,
    vector_v,
):
    clips, tiles = sizes
    levels = make_levels(clips, tiles)
    tile = lax.axis_index("tile")
    unused, frames, local = codes.shape
    own_frames = frames // tiles
    positions = local * tiles
    both = ("clip", "tile")

    vec_rows = vectors.shape[1] // tiles
    vec_own = cut(vectors, tile, vec_rows, 1).T.astype(bf16)
    vec_own = jnp.pad(vec_own, ((0, 0), (0, LANES - vec_own.shape[1])))
    row_part = weights.shape[0] // tiles
    part = cut(weights, tile, row_part, 0).astype(bf16)

    def slab(number):
        return part[:, STARTS[number] : STARTS[number + 1]]

    def fetch(pieces):
        whole = lax.all_gather(jnp.concatenate(pieces, 1), both, axis=0, tiled=True)
        parts, begin = [], 0
        for piece in pieces:
            parts.append(whole[:, begin : begin + piece.shape[1]])
            begin += piece.shape[1]
        return parts

    embed_table, space_in, vec_cols = fetch([slab(6), slab(0), vec_own])
    space_out, time_in, time_out = fetch([slab(1), slab(2), slab(3)])
    feed_up, feed_down, head_table = fetch([slab(4), slab(5), slab(7)])
    vecs = vec_cols[:, : vectors.shape[0]].T.astype(f32)

    domain_hot = (domains[:, None] == jnp.arange(NDOM)[None, :]).astype(f32)
    masked_clip = jnp.sum(mask.astype(f32), axis=(1, 2))
    counts = jnp.sum(domain_hot * masked_clip[:, None], 0)
    for name in ("core", "x", "inner", "outer"):
        counts = levels[name].sum(counts)
    inverse = 1.0 / jnp.maximum(counts, 1.0)
    clip_weight = jnp.sum(domain_hot * inverse[None, :]) / NDOM

    packed = lax.all_gather(codes[0] + V * mask[0], "tile", axis=1, tiled=True)
    packed = cut(packed, tile, own_frames, 0)
    frame_codes, frame_mask = packed % V, packed // V
    action_hot = (actions[0][:, None] == jnp.arange(ACTIONS)[None, :]).astype(f32)
    action_add = jnp.dot(action_hot, vecs[9:], precision=highest)

    def embed(code, masked, action_rows, span):
        rows = code.size
        hot = (code.reshape(rows)[:, None] == jnp.arange(V)[None, :]).astype(bf16)
        masked = masked.reshape(rows, 1).astype(f32)
        looked = dot_nt(hot, embed_table)
        added = jnp.repeat(action_rows, span, axis=0)
        return (hot, masked, masked * vecs[8] + (1.0 - masked) * looked + added)

    frame_hot, frame_col, frame_zero = embed(
        frame_codes, frame_mask, cut(action_add, tile, own_frames, 0), positions
    )
    code_hot, mask_col, stream_zero = embed(codes[0], mask[0], action_add, local)

    stat_s = norm_stats(frame_zero)
    normed_s = norm_apply(frame_zero, stat_s, vecs[0], vecs[4])
    projected_s = dot_nn(normed_s, space_in).astype(bf16)
    mixed_s = attend_space(projected_s)

    def flip(array, step):
        pairs = [(source, (source + step) % tiles) for source in range(tiles)]
        return lax.ppermute(array, "tile", pairs)

    def to_positions(array):
        cube = array.reshape(own_frames, tiles, local, D).swapaxes(0, 1)
        whole = jnp.zeros((tiles, own_frames, local, D), bf16)
        for step in range(tiles):
            piece = lax.dynamic_index_in_dim(cube, (tile + step) % tiles, 0)
            if step:
                piece = flip(piece, step)
            whole = lax.dynamic_update_slice_in_dim(whole, piece, (tile - step) % tiles, 0)
        return whole.reshape(frames * local, D)

    def to_frames(array):
        cube = array.reshape(tiles, own_frames, local, D)
        whole = jnp.zeros((tiles, own_frames, local, D), bf16)
        for step in range(tiles):
            piece = lax.dynamic_index_in_dim(cube, (tile + step) % tiles, 0)
            if step:
                piece = flip(piece, step)
            whole = lax.dynamic_update_slice_in_dim(whole, piece, (tile - step) % tiles, 0)
        return whole.swapaxes(0, 1).reshape(own_frames * positions, D)

    attended_s = to_positions(mixed_s)
    stream_one = stream_zero + dot_nn(attended_s, space_out)

    stat_t = norm_stats(stream_one)
    normed_t = norm_apply(stream_one, stat_t, vecs[1], vecs[5])
    projected_t = dot_nn(normed_t, time_in).astype(bf16)
    attended_t = attend_time(projected_t, frames)
    stream_two = stream_one + dot_nn(attended_t, time_out)

    stat_f = norm_stats(stream_two)
    normed_f = norm_apply(stream_two, stat_f, vecs[2], vecs[6])
    activated, slope = gelu_pair(dot_nn(normed_f, feed_up))
    activated = activated.astype(bf16)
    stream_three = stream_two + dot_nt(activated, feed_down)

    stat_o = norm_stats(stream_three)
    normed_o = norm_apply(stream_three, stat_o, vecs[3], vecs[7])
    logits = dot_nn(normed_o, head_table)
    largest = jnp.max(logits, -1, keepdims=True)
    log_sum = largest + jnp.log(jnp.sum(jnp.exp(logits - largest), -1, keepdims=True))
    code_float = code_hot.astype(f32)
    picked = jnp.sum(logits * code_float, -1, keepdims=True)
    ce_part = domain_hot[0] * jnp.sum((log_sum - picked) * mask_col)
    token_weight = clip_weight * mask_col
    grad_logits = (token_weight * (jnp.exp(logits - log_sum) - code_float)).astype(bf16)

    reducer = Reducer(levels)
    head_part = reducer.start(normed_o, grad_logits)
    grad_stream, gain_o, offset_o = norm_back(
        stream_three, stat_o, vecs[3], dot_nt(grad_logits, head_table)
    )
    branch = grad_stream.astype(bf16)
    down_part = reducer.start(branch, activated)
    grad_up_rows = (dot_nn(branch, feed_down) * slope).astype(bf16)
    up_part = reducer.start(normed_f, grad_up_rows)
    back_x, gain_f, offset_f = norm_back(stream_two, stat_f, vecs[2], dot_nt(grad_up_rows, feed_up))
    grad_stream = grad_stream + back_x
    branch = grad_stream.astype(bf16)
    time_out_part = reducer.start(attended_t, branch)
    grad_mixed = dot_nt(branch, time_out).astype(bf16)
    time_grad = attend_time_back(projected_t, grad_mixed, frames)
    time_in_part = reducer.start(normed_t, time_grad)
    back_x, gain_t, offset_t = norm_back(stream_one, stat_t, vecs[1], dot_nt(time_grad, time_in))
    grad_stream = grad_stream + back_x
    branch = grad_stream.astype(bf16)
    grad_mixed = to_frames(dot_nt(branch, space_out).astype(bf16))
    space_out_part = reducer.start(attended_s, branch)
    space_grad = attend_space_back(projected_s, grad_mixed)
    space_in_part = reducer.start(normed_s, space_grad)
    back_x, gain_s, offset_s = norm_back(frame_zero, stat_s, vecs[0], dot_nt(space_grad, space_in))

    embed_former = jnp.concatenate([(1.0 - mask_col) * grad_stream, (1.0 - frame_col) * back_x], 0)
    embed_part = reducer.start(
        embed_former.astype(bf16), jnp.concatenate([code_hot, frame_hot], 0)
    )
    grad_mask = jnp.sum(mask_col * grad_stream, 0) + jnp.sum(frame_col * back_x, 0)
    frame_sum = jnp.sum(grad_stream.reshape(frames, local, D), 1)
    own_sum = jnp.sum(back_x.reshape(own_frames, positions, D), 1)
    own_hot = cut(action_hot, tile, own_frames, 0)
    grad_action = jnp.dot(action_hot.T, frame_sum, precision=highest) + jnp.dot(
        own_hot.T, own_sum, precision=highest
    )
    grad_v = jnp.concatenate(
        [
            jnp.stack(
                [gain_s, gain_t, gain_f, gain_o, offset_s, offset_t, offset_f, offset_o, grad_mask]
            ),
            grad_action,
        ],
        0,
    )
    vec_count = grad_v.shape[0]
    grad_v = jnp.pad(grad_v, ((0, LANES - vec_count), (0, 0))).T
    vec_part = reducer.start_vector(grad_v)

    owned = [None] * 8
    owned_v = None
    groups = [
        [(7, head_part), (5, down_part)],
        [(4, up_part)],
        [(3, time_out_part), (2, time_in_part)],
        [(1, space_out_part), (0, space_in_part), (6, embed_part), (8, vec_part)],
    ]
    for group in groups:
        summed = reducer.finish([started for _, started in group])
        widths = [started[0] for number, started in group if number < 8]
        wholes = reducer.spread(summed[:, : sum(widths)], widths)
        for (number, _), whole in zip(group, wholes):
            owned[number] = whole
        if group[-1][0] == 8:
            owned_v = summed[:, sum(widths) :][:, :vec_count].T

    rows = weights.shape[0]
    outers = []
    for number in range(8):
        block = owned[number].reshape(rows // BLOCK, BLOCK, WIDTHS[number])
        outers.append(jnp.einsum("bic,bkc->bik", block, block, preferred_element_type=f32))
    outers = jnp.stack(outers)
    diagonal = jnp.eye(BLOCK, dtype=f32)
    squares = jnp.sum(outers * diagonal) + jnp.sum(owned_v * owned_v)
    sums = jnp.concatenate([ce_part, (squares / tiles)[None]])
    for name in ("core", "x", "inner", "outer"):
        sums = levels[name].sum(sums)
    ce_total = sums[:NDOM]
    grad_norm = jnp.sqrt(sums[NDOM])
    clip_scale = 1.0 / jnp.maximum(grad_norm, 1.0)
    new_weights, new_weight_m, new_weight_v = update_weights(
        clip_scale, jnp.concatenate(owned, 1), weights, weight_m, weight_v, bases
    )
    new_stats, new_bases = turn_bases(clip_scale, outers, stats, bases)
    new_vectors, new_vector_m, new_vector_v = adam_update(
        vectors, vector_m, vector_v, owned_v * clip_scale
    )
    loss_terms = jnp.stack([ce_total, counts])
    return (
        loss_terms,
        grad_norm,
        new_weights,
        new_weight_m,
        new_weight_v,
        new_stats,
        new_bases,
        new_vectors,
        new_vector_m,
        new_vector_v,
    )


def solution(mesh):
    sizes = (mesh.shape["clip"], mesh.shape["tile"])
    placed = (
        P("clip", None, "tile"),
        P("clip", None, "tile"),
        P("clip", None),
        P("clip"),
        P("clip", None),
        P("clip", None),
        P("clip", None),
        P(None, "clip", None),
        P(None, "clip", None),
        P(None, "clip"),
        P(None, "clip"),
        P(None, "clip"),
    )
    return jax.shard_map(
        partial(body, sizes),
        mesh=mesh,
        in_specs=placed,
        out_specs=(
            P(),
            P(),
            P("clip", None),
            P("clip", None),
            P("clip", None),
            P(None, "clip", None),
            P(None, "clip", None),
            P(None, "clip"),
            P(None, "clip"),
            P(None, "clip"),
        ),
        check_vma=False,
    )
```
